32 devices in a mesh: region: 8 (over y, x, core), shard: 4 (over z).
Axes of the slice: x: 2, y: 2, z: 4, core: 2. Of those that a mesh axis runs over, the one named last changes fastest.
Arguments:
- state_anom: float32 [32768, 256], P(('region', 'shard')), may hold values from -6 to 6
- state_mean: float32 [32768], P(('region', 'shard')), may hold values from -6 to 6
- obs_anom: float32 [16, 512, 256], P('region', 'shard'), may hold values from -6 to 6
- obs_depart: float32 [16, 512], P('region', 'shard'), may hold values from -6 to 6
- obs_var: float32 [16, 512], P('region', 'shard'), may hold values from 0.5 to 2
- taper_levels: float32 [8], replicated, may hold values from 0 to 1
- state_taper: int32 [256, 64], P(('region', 'shard')), may hold values from 0 to 7
- obs_taper: int32 [64, 64], P('region'), may hold values from 0 to 7
- batch_order: int32 [3], replicated, may hold values from 0 to 15, as said below
Outputs:
- post_anom: float32 [32768, 256], P(('region', 'shard'))
- post_mean: float32 [32768], P(('region', 'shard'))
- post_obs_anom: float32 [16, 512, 256], P('region', 'shard')
- post_obs_depart: float32 [16, 512], P('region', 'shard')
The draws below stay inside these ranges and needn't reach their ends.
Inputs may be any that keep to these rules, and one draw needn't show every extreme that they name: `batch_order`: 3 distinct batch numbers; batch q lies in region q // 2; the first and the last batch number both occur.
All inputs are finite; a program needn't handle non-finite values.
Results may differ from the reference program's by a relative error of at most 0.0001.
Values sent between devices are 32-bit elements; how exact they have to be, the bound alone decides.
A program may use at most 64 MiB of HBM per device.

```python
import math
import jax
import jax.numpy as jnp
from jax import lax

M = 256
P_SIZE = 512
TAPER_BLOCK = 128
LEVELS = 8
NB = 3
ROWS_DEV = 1024
STATE = 32768
NOBSB = 16
NOBS = 8192


def draw_batch_order(key, part):
    inner = jax.random.permutation(jax.random.fold_in(key, 11), NOBSB - 2)[:NB - 2] + 1
    chosen = jnp.concatenate([jnp.array([0, NOBSB - 1], jnp.int32), inner.astype(jnp.int32)])
    return jax.random.permutation(jax.random.fold_in(key, 12), chosen).astype(jnp.int32)


def place_ends(result, stream_key, least, largest):
    place = [jax.random.randint(jax.random.fold_in(stream_key, axis), (), 0, length) for axis, length in enumerate(result.shape)]
    widest = result.shape.index(max(result.shape))
    neighbour = place[:widest] + [(place[widest] + 1) % result.shape[widest]] + place[widest + 1:]
    return result.at[tuple(place)].set(least).at[tuple(neighbour)].set(largest)


def block_levels(key, dims, cuts, least, largest):
    def one(axis_at, blocks):
        heights = jax.random.uniform(jax.random.fold_in(jax.random.fold_in(key, 6), axis_at), (blocks,), jnp.float32, least / len(cuts), largest / len(cuts))
        return jnp.repeat(jnp.exp(heights), dims[axis_at] // blocks).reshape((-1,) + (1,) * (len(dims) - axis_at - 1))

    level = one(*cuts[0])
    for cut in cuts[1:]:
        level = level * one(*cut)
    return level


def gaussian(rng, shape, deviation, bound, cuts=(), held_as=jnp.bfloat16):
    drawn = deviation * jax.random.normal(rng, shape, jnp.float32)
    if cuts:
        drawn = drawn * block_levels(rng, shape, cuts, -0.22, 0.18)
    return jnp.clip(drawn, -bound, bound).astype(held_as)


def setup_inputs(seed: int = 0) -> dict:
    keys = jax.random.split(jax.random.key(seed), 10)
    state_anom = gaussian(keys[0], (STATE, M), 1.0, 6.0, ((0, 32),), jnp.float32)
    state_mean = gaussian(keys[1], (STATE,), 1.0, 6.0, ((0, 32),), jnp.float32)
    obs_anom = gaussian(keys[2], (NOBSB, P_SIZE, M), 1.0, 6.0, ((0, 8), (1, 4)), jnp.float32)
    obs_depart = gaussian(keys[3], (NOBSB, P_SIZE), 1.0, 6.0, ((0, 8), (1, 4)), jnp.float32)
    obs_var = jnp.clip(jnp.exp(math.log(2.0) - 1.3862944 * jax.random.uniform(keys[4], (NOBSB, P_SIZE), jnp.float32) ** block_levels(keys[4], (NOBSB, P_SIZE), ((0, 8), (1, 4)), -0.2, 0.2)), 0.5, 2.0)
    taper_levels = jnp.clip(jax.random.uniform(keys[5], (LEVELS,), jnp.float32, 0.0, 1.0), 0.0, 1.0)
    state_taper = place_ends(jax.random.randint(keys[6], (STATE // TAPER_BLOCK, NOBS // TAPER_BLOCK), 0, LEVELS), jax.random.fold_in(keys[6], 1), 0, LEVELS - 1).astype(jnp.int32)
    obs_taper = place_ends(jax.random.randint(keys[7], (NOBS // TAPER_BLOCK, NOBS // TAPER_BLOCK), 0, LEVELS), jax.random.fold_in(keys[7], 1), 0, LEVELS - 1).astype(jnp.int32)
    batch_order = draw_batch_order(jax.random.fold_in(keys[9], 71), 0)
    return dict(state_anom=state_anom, state_mean=state_mean, obs_anom=obs_anom, obs_depart=obs_depart, obs_var=obs_var, taper_levels=taper_levels, state_taper=state_taper, obs_taper=obs_taper, batch_order=batch_order)


highest = lax.Precision.HIGHEST

def factorize(anomalies, departs, variances):
    product = jnp.dot(anomalies.astype(jnp.float32), anomalies.T.astype(jnp.float32), precision=highest, preferred_element_type=jnp.float32)
    system = product / (M - 1) + jnp.diag(variances)
    lower_factor = jnp.linalg.cholesky(system)
    shifted = lower_factor + jnp.diag(jnp.sqrt(variances))
    solved = lax.linalg.triangular_solve(shifted, anomalies, left_side=True, lower=True)
    increments = lax.linalg.triangular_solve(lower_factor, solved, left_side=True, lower=True, transpose_a=True)
    first = lax.linalg.triangular_solve(lower_factor, departs[:, None], left_side=True, lower=True)
    weights = lax.linalg.triangular_solve(lower_factor, first, left_side=True, lower=True, transpose_a=True)
    return (increments, weights[:, 0])

def regress(rows, batch_rows, taper, increments, weights):
    count_rows = rows.shape[0]
    blocks = P_SIZE // TAPER_BLOCK
    covar = jnp.dot(rows.astype(jnp.float32), batch_rows.T.astype(jnp.float32), precision=highest, preferred_element_type=jnp.float32) / (M - 1)
    covar = covar.reshape(count_rows // TAPER_BLOCK, TAPER_BLOCK, blocks, TAPER_BLOCK) * taper[:, None, :, None]
    covar = covar.reshape(count_rows, P_SIZE)
    delta_rows = jnp.dot(covar.astype(jnp.float32), increments.astype(jnp.float32), precision=highest, preferred_element_type=jnp.float32)
    delta_mean = jnp.dot(covar.astype(jnp.float32), weights.astype(jnp.float32), precision=highest, preferred_element_type=jnp.float32)
    return (delta_rows, delta_mean)

def reference(state_anom, state_mean, obs_anom, obs_depart, obs_var, taper_levels, state_taper, obs_taper, batch_order):
    blocks = P_SIZE // TAPER_BLOCK
    groups = STATE // ROWS_DEV
    anomaly = state_anom.reshape(groups, ROWS_DEV, M)
    mean_state = state_mean.reshape(groups, ROWS_DEV)
    obs_now = obs_anom
    depart_now = obs_depart
    for section_idx in range(NB):
        batch_id = batch_order[section_idx]
        batch_rows = lax.dynamic_index_in_dim(obs_now, batch_id, 0, keepdims=False)
        departs = lax.dynamic_index_in_dim(depart_now, batch_id, 0, keepdims=False)
        variances = lax.dynamic_index_in_dim(obs_var, batch_id, 0, keepdims=False)
        increments, weights = factorize(batch_rows, departs, variances)
        state_cols = lax.dynamic_slice_in_dim(state_taper, batch_id * blocks, blocks, 1)
        state_weights = taper_levels[state_cols].reshape(groups, ROWS_DEV // TAPER_BLOCK, blocks)
        obs_cols = lax.dynamic_slice_in_dim(obs_taper, batch_id * blocks, blocks, 1)
        obs_weights = taper_levels[obs_cols].reshape(NOBSB, P_SIZE // TAPER_BLOCK, blocks)

        def state_group(items):
            rows, means, taper = items
            delta_rows, delta_mean = regress(rows, batch_rows, taper, increments, weights)
            return (rows - delta_rows, means + delta_mean)

        def obs_group(items):
            rows, departs_here, taper = items
            delta_rows, delta_mean = regress(rows, batch_rows, taper, increments, weights)
            return (rows - delta_rows, departs_here - delta_mean)
        anomaly, mean_state = lax.map(state_group, (anomaly, mean_state, state_weights))
        obs_now, depart_now = lax.map(obs_group, (obs_now, depart_now, obs_weights))
    return (anomaly.reshape(STATE, M), mean_state.reshape(STATE), obs_now, depart_now)
```

```python
import jax
import jax.numpy as jnp
from jax import lax
from jax.experimental import pallas as pl
from jax.experimental.pallas import tpu as pltpu
from jax.sharding import PartitionSpec as P

TAPER_BLOCK = 128
LANES = 128
PANEL = 16
highest = lax.Precision.HIGHEST
f32 = jnp.float32
bf16 = jnp.bfloat16


def dot(a, b, dims=((1,), (0,))):
    return lax.dot_general(a, b, (dims, ((), ())), precision=highest, preferred_element_type=f32)


def split2(x):
    hi = x.astype(bf16)
    return hi, (x - hi.astype(f32)).astype(bf16)


def split3(x):
    hi = x.astype(bf16).astype(f32)
    rest = x - hi
    mid = rest.astype(bf16).astype(f32)
    return hi, mid, rest - mid


def dot3(a, b_hi, b_lo, dims=((1,), (0,))):
    hi, lo = split2(a)

    def one(u, v):
        return lax.dot_general(u, v, (dims, ((), ())), preferred_element_type=f32)

    return one(hi, b_hi) + (one(hi, b_lo) + one(lo, b_hi))


def factor_block(sgh, roots):
    rows = lax.broadcasted_iota(jnp.int32, (PANEL, LANES), 0)
    for start in range(0, TAPER_BLOCK, PANEL):
        panel = sgh[start : start + PANEL, :]
        cols = [
            jnp.broadcast_to(panel[:, start + t : start + t + 1], (PANEL, LANES))
            for t in range(PANEL)
        ]
        parts = [panel[:, LANES * q : LANES * (q + 1)] for q in range(3)]
        root = roots[start : start + PANEL, :]
        for r in range(PANEL):
            pivot = cols[r][r : r + 1, :]
            inv = lax.rsqrt(pivot)
            column = cols[r] * inv
            for t in range(r + 1, PANEL):
                cols[t] = cols[t] - column * column[t : t + 1, :]
            below = jnp.where(rows > r, column, 0.0)
            shifted = 1.0 / (pivot * inv + root[r : r + 1, :])
            for q, scale in enumerate((inv, inv, shifted)):
                done = parts[q][r : r + 1, :] * scale
                parts[q] = jnp.where(rows == r, done, parts[q] - below * done)
        solved = jnp.concatenate(parts, axis=1)
        sgh[start : start + PANEL, :] = solved
        after = start + PANEL
        if after < TAPER_BLOCK:
            a, b, c = split3(parts[0])
            left = jnp.concatenate([a, a, b, a, b, c, jnp.zeros((32, LANES), f32)], axis=0)
            x, y, z = (v.astype(bf16) for v in split3(solved))
            right = jnp.concatenate([x, y, x, z, y, x, jnp.zeros((32, 3 * LANES), bf16)], axis=0)
            left = left.T[after:, :].astype(bf16)
            sgh[after:, :] = sgh[after:, :] - jnp.dot(left, right, preferred_element_type=f32)


def analysis_kernel(
    members, state_in, obs_in, batch_in, tw_state, tw_obs, tw_batch, state, obs, batch, work, sgh, roots, inverses, y_hi, y_lo, z, z_hi, z_lo
):
    steps, size, width = batch_in.shape
    blocks = size // TAPER_BLOCK
    state[...] = state_in[...]
    obs[...] = obs_in[...]
    for k in range(steps):
        batch[k] = batch_in[k]
    eye = (
        lax.broadcasted_iota(jnp.int32, (TAPER_BLOCK, LANES), 0)
        == lax.broadcasted_iota(jnp.int32, (TAPER_BLOCK, LANES), 1)
    ).astype(f32)
    lane = lax.broadcasted_iota(jnp.int32, (TAPER_BLOCK, LANES), 1)
    extra = size + members

    def one_batch(k, carry):
        y = batch[k, :, :members]
        hi, lo = split2(y)
        y_hi[...] = hi
        y_lo[...] = lo
        work[:, size:] = batch[k]
        for j in range(blocks):
            here = y[j * TAPER_BLOCK : (j + 1) * TAPER_BLOCK]
            work[j * TAPER_BLOCK : (j + 1) * TAPER_BLOCK, :size] = dot(here, y, ((1,), (1,))) / (members - 1)

        def eliminate(j, carry):
            top = pl.multiple_of(j * TAPER_BLOCK, TAPER_BLOCK)
            mine = pl.ds(top, TAPER_BLOCK)
            variance = jnp.broadcast_to(batch[k, mine, members + 1 : members + 2], (TAPER_BLOCK, LANES))
            roots[...] = jnp.sqrt(variance)
            sgh[:, :LANES] = work[mine, mine] + eye * variance
            sgh[:, LANES : 2 * LANES] = eye
            sgh[:, 2 * LANES :] = eye
            factor_block(sgh, roots)
            inverse = sgh[:, LANES : 2 * LANES]
            inverses[j] = inverse
            work[mine, :size] = dot(inverse, work[mine, :size])
            work[mine, size:extra] = dot(sgh[:, 2 * LANES :], work[mine, size:extra])
            work[mine, extra:] = dot(inverse, work[mine, extra:])

            def trail(i, carry):
                lower = pl.ds(pl.multiple_of(i * TAPER_BLOCK, TAPER_BLOCK), TAPER_BLOCK)
                work[lower, :] = work[lower, :] - dot(work[mine, lower].T, work[mine, :])
                return carry

            return lax.fori_loop(j + 1, blocks, trail, carry)

        lax.fori_loop(0, blocks, eliminate, 0)

        def back(step, carry):
            j = blocks - 1 - step
            mine = pl.ds(pl.multiple_of(j * TAPER_BLOCK, TAPER_BLOCK), TAPER_BLOCK)

            def gather(i, acc):
                lower = pl.ds(pl.multiple_of(i * TAPER_BLOCK, TAPER_BLOCK), TAPER_BLOCK)
                return acc - dot(work[mine, lower], z[lower, :])

            acc = lax.fori_loop(j + 1, blocks, gather, work[mine, size:])
            z[mine, :] = dot(inverses[j].T, acc)
            return carry

        lax.fori_loop(0, blocks, back, 0)
        for j in range(blocks):
            mine = slice(j * TAPER_BLOCK, (j + 1) * TAPER_BLOCK)
            tail = jnp.where(lane == 0, z[mine, members:], 0.0)
            full = jnp.concatenate([z[mine, :members], tail], axis=1)
            hi, lo = split2(full)
            z_hi[mine, :] = hi
            z_lo[mine, :] = lo

        def updated(x, weights):
            covar = dot3(x[:, :members], y_hi[...], y_lo[...], ((1,), (1,))) * weights
            return x - dot3(covar, z_hi[...], z_lo[...])

        def state_block(i, carry):
            mine = pl.ds(pl.multiple_of(i * TAPER_BLOCK, TAPER_BLOCK), TAPER_BLOCK)
            state[mine, :] = updated(state[mine, :], tw_state[k, pl.ds(i, 1), :])
            return carry

        lax.fori_loop(0, state.shape[0] // TAPER_BLOCK, state_block, 0)
        groups = tw_obs.shape[1]
        high = obs.shape[0] // groups
        for g in range(groups):
            mine = slice(g * high, (g + 1) * high)
            obs[mine, :] = updated(obs[mine, :], tw_obs[k, g : g + 1, :])

        def later(i, carry):
            which = i // blocks
            mine = pl.ds(pl.multiple_of(lax.rem(i, blocks) * TAPER_BLOCK, TAPER_BLOCK), TAPER_BLOCK)
            batch[which, mine, :] = updated(batch[which, mine, :], tw_batch[k, pl.ds(i, 1), :])
            return carry

        lax.fori_loop((k + 1) * blocks, steps * blocks, later, 0)
        return carry

    lax.fori_loop(0, steps, one_batch, 0)


def analyse(members, state, obs, batch, tw_state, tw_obs, tw_batch):
    steps, size, width = batch.shape
    blocks = size // TAPER_BLOCK
    vmem = pl.BlockSpec(memory_space=pltpu.VMEM)

    def kernel(*refs):
        analysis_kernel(members, *refs)

    return pl.pallas_call(
        kernel,
        out_shape=(jax.ShapeDtypeStruct(state.shape, f32), jax.ShapeDtypeStruct(obs.shape, f32)),
        in_specs=[vmem] * 6,
        out_specs=(vmem, vmem),
        scratch_shapes=[
            pltpu.VMEM(batch.shape, f32),
            pltpu.VMEM((size, size + width), f32),
            pltpu.VMEM((TAPER_BLOCK, 3 * LANES), f32),
            pltpu.VMEM((TAPER_BLOCK, LANES), f32),
            pltpu.VMEM((blocks, TAPER_BLOCK, LANES), f32),
            pltpu.VMEM((size, members), bf16),
            pltpu.VMEM((size, members), bf16),
            pltpu.VMEM((size, width), f32),
            pltpu.VMEM((size, width), bf16),
            pltpu.VMEM((size, width), bf16),
        ],
        compiler_params=pltpu.CompilerParams(vmem_limit_bytes=48 * 1024 * 1024),
    )(state, obs, batch, tw_state, tw_obs, tw_batch)


def lookup(levels, index):
    onehot = (index[..., None] == jnp.arange(levels.shape[0], dtype=jnp.int32)).astype(f32)
    return jnp.sum(onehot * levels, axis=-1)


def per_device(
    state_anom, state_mean, obs_anom, obs_depart, obs_var, taper_levels, state_taper, obs_taper, batch_order
):
    region, shard = lax.axis_index("region"), lax.axis_index("shard")
    per_region, pieces, members = obs_anom.shape
    steps = batch_order.shape[0]
    size = pieces * lax.axis_size("shard")
    blocks = size // TAPER_BLOCK

    def columns(weights):
        return jnp.repeat(weights, TAPER_BLOCK, axis=-1) / (members - 1)

    wanted = (batch_order[:, None] * blocks + jnp.arange(blocks, dtype=jnp.int32)).reshape(-1)
    state_weights = lookup(taper_levels, jnp.take(state_taper, wanted, axis=1))
    tw_state = columns(state_weights.reshape(-1, steps, blocks)).transpose(1, 0, 2)
    obs_weights = lookup(taper_levels, jnp.take(obs_taper, wanted, axis=1))
    high = min(pieces, TAPER_BLOCK)
    group_rows = jnp.arange(per_region * pieces // high, dtype=jnp.int32) * high
    group_block = (group_rows // pieces * size + shard * pieces + group_rows % pieces) // TAPER_BLOCK
    mine = jnp.take(obs_weights, group_block, axis=0)
    tw_obs = columns(mine.reshape(-1, steps, blocks)).transpose(1, 0, 2)

    weight_rows = jnp.repeat(mine, high, axis=0).reshape(per_region, pieces, steps * blocks)
    pad = jnp.zeros((per_region, pieces, LANES - 2 - steps * blocks), f32)
    table = jnp.concatenate([obs_anom, obs_depart[..., None], obs_var[..., None], weight_rows, pad], axis=-1)
    share = jnp.take(table, batch_order % per_region, axis=0)
    owned = (batch_order // per_region == region)[:, None, None]
    share = lax.psum(jnp.where(owned, share, 0.0), "region")
    batch = lax.all_gather(share, "shard", axis=1, tiled=True)

    between = batch[:, ::TAPER_BLOCK, members + 2 : members + 2 + steps * blocks]
    tw_batch = columns(between.reshape(steps * blocks, steps, blocks)).transpose(1, 0, 2)

    def widened(rows, column):
        pad = jnp.zeros((rows.shape[0], LANES - 1), f32)
        return jnp.concatenate([rows, column[:, None], pad], axis=1)

    state, obs = analyse(
        members,
        widened(state_anom, -state_mean),
        widened(obs_anom.reshape(-1, members), obs_depart.reshape(-1)),
        batch,
        tw_state,
        tw_obs,
        tw_batch,
    )
    return (
        state[:, :members],
        -state[:, members],
        obs[:, :members].reshape(obs_anom.shape),
        obs[:, members].reshape(obs_depart.shape),
    )


def solution(mesh):
    placed = (
        P(("region", "shard"), None),
        P(("region", "shard")),
        P("region", "shard", None),
        P("region", "shard"),
        P("region", "shard"),
        P(),
        P(("region", "shard"), None),
        P("region", None),
        P(),
    )
    return jax.shard_map(
        per_device,
        mesh=mesh,
        in_specs=placed,
        out_specs=(
            P(("region", "shard"), None),
            P(("region", "shard")),
            P("region", "shard", None),
            P("region", "shard"),
        ),
        check_vma=False,
    )
```

```python
import jax
import jax.numpy as jnp
from jax import lax
from jax.experimental import pallas as pl
from jax.experimental.pallas import tpu as pltpu
from jax.sharding import PartitionSpec as P

TAPER_BLOCK = 128
LANES = 128
PANEL = 16
highest = lax.Precision.HIGHEST
f32 = jnp.float32
bf16 = jnp.bfloat16


def dot(a, b, dims=((1,), (0,))):
    return lax.dot_general(a, b, (dims, ((), ())), precision=highest, preferred_element_type=f32)


def split2(x):
    hi = x.astype(bf16)
    return hi, (x - hi.astype(f32)).astype(bf16)


def split3(x):
    hi = x.astype(bf16).astype(f32)
    rest = x - hi
    mid = rest.astype(bf16).astype(f32)
    return hi, mid, rest - mid


def dot3(a, b_hi, b_lo, dims=((1,), (0,))):
    hi, lo = split2(a)

    def one(u, v):
        return lax.dot_general(u, v, (dims, ((), ())), preferred_element_type=f32)

    return one(hi, b_hi) + (one(hi, b_lo) + one(lo, b_hi))


def factor_block(sgh, roots):
    rows = lax.broadcasted_iota(jnp.int32, (PANEL, LANES), 0)
    for start in range(0, TAPER_BLOCK, PANEL):
        panel = sgh[start : start + PANEL, :]
        cols = [
            jnp.broadcast_to(panel[:, start + t : start + t + 1], (PANEL, LANES))
            for t in range(PANEL)
        ]
        parts = [panel[:, LANES * q : LANES * (q + 1)] for q in range(3)]
        root = roots[start : start + PANEL, :]
        for r in range(PANEL):
            pivot = cols[r][r : r + 1, :]
            inv = lax.rsqrt(pivot)
            column = cols[r] * inv
            for t in range(r + 1, PANEL):
                cols[t] = cols[t] - column * column[t : t + 1, :]
            below = jnp.where(rows > r, column, 0.0)
            shifted = 1.0 / (pivot * inv + root[r : r + 1, :])
            for q, scale in enumerate((inv, inv, shifted)):
                done = parts[q][r : r + 1, :] * scale
                parts[q] = jnp.where(rows == r, done, parts[q] - below * done)
        solved = jnp.concatenate(parts, axis=1)
        sgh[start : start + PANEL, :] = solved
        after = start + PANEL
        if after < TAPER_BLOCK:
            a, b, c = split3(parts[0])
            left = jnp.concatenate([a, a, b, a, b, c, jnp.zeros((32, LANES), f32)], axis=0)
            x, y, z = (v.astype(bf16) for v in split3(solved))
            right = jnp.concatenate([x, y, x, z, y, x, jnp.zeros((32, 3 * LANES), bf16)], axis=0)
            left = left.T[after:, :].astype(bf16)
            sgh[after:, :] = sgh[after:, :] - jnp.dot(left, right, preferred_element_type=f32)


def analysis_kernel(
    members, state_in, obs_in, batch_in, tw_state, tw_obs, tw_batch, state, obs, batch, work, sgh, roots, inverses, y_hi, y_lo, z, z_hi, z_lo
):
    steps, size, width = batch_in.shape
    blocks = size // TAPER_BLOCK
    state[...] = state_in[...]
    obs[...] = obs_in[...]
    for k in range(steps):
        batch[k] = batch_in[k]
    eye = (
        lax.broadcasted_iota(jnp.int32, (TAPER_BLOCK, LANES), 0)
        == lax.broadcasted_iota(jnp.int32, (TAPER_BLOCK, LANES), 1)
    ).astype(f32)
    lane = lax.broadcasted_iota(jnp.int32, (TAPER_BLOCK, LANES), 1)
    extra = size + members

    def one_batch(k, carry):
        y = batch[k, :, :members]
        hi, lo = split2(y)
        y_hi[...] = hi
        y_lo[...] = lo
        work[:, size:] = batch[k]
        for j in range(blocks):
            here = y[j * TAPER_BLOCK : (j + 1) * TAPER_BLOCK]
            work[j * TAPER_BLOCK : (j + 1) * TAPER_BLOCK, :size] = dot(here, y, ((1,), (1,))) / (members - 1)

        def eliminate(j, carry):
            top = pl.multiple_of(j * TAPER_BLOCK, TAPER_BLOCK)
            mine = pl.ds(top, TAPER_BLOCK)
            variance = jnp.broadcast_to(batch[k, mine, members + 1 : members + 2], (TAPER_BLOCK, LANES))
            roots[...] = jnp.sqrt(variance)
            sgh[:, :LANES] = work[mine, mine] + eye * variance
            sgh[:, LANES : 2 * LANES] = eye
            sgh[:, 2 * LANES :] = eye
            factor_block(sgh, roots)
            inverse = sgh[:, LANES : 2 * LANES]
            inverses[j] = inverse
            work[mine, :size] = dot(inverse, work[mine, :size])
            work[mine, size:extra] = dot(sgh[:, 2 * LANES :], work[mine, size:extra])
            work[mine, extra:] = dot(inverse, work[mine, extra:])

            def trail(i, carry):
                lower = pl.ds(pl.multiple_of(i * TAPER_BLOCK, TAPER_BLOCK), TAPER_BLOCK)
                work[lower, :] = work[lower, :] - dot(work[mine, lower].T, work[mine, :])
                return carry

            return lax.fori_loop(j + 1, blocks, trail, carry)

        lax.fori_loop(0, blocks, eliminate, 0)

        def back(step, carry):
            j = blocks - 1 - step
            mine = pl.ds(pl.multiple_of(j * TAPER_BLOCK, TAPER_BLOCK), TAPER_BLOCK)

            def gather(i, acc):
                lower = pl.ds(pl.multiple_of(i * TAPER_BLOCK, TAPER_BLOCK), TAPER_BLOCK)
                return acc - dot(work[mine, lower], z[lower, :])

            acc = lax.fori_loop(j + 1, blocks, gather, work[mine, size:])
            z[mine, :] = dot(inverses[j].T, acc)
            return carry

        lax.fori_loop(0, blocks, back, 0)
        for j in range(blocks):
            mine = slice(j * TAPER_BLOCK, (j + 1) * TAPER_BLOCK)
            tail = jnp.where(lane == 0, z[mine, members:], 0.0)
            full = jnp.concatenate([z[mine, :members], tail], axis=1)
            hi, lo = split2(full)
            z_hi[mine, :] = hi
            z_lo[mine, :] = lo

        def updated(x, weights):
            covar = dot3(x[:, :members], y_hi[...], y_lo[...], ((1,), (1,))) * weights
            return x - dot3(covar, z_hi[...], z_lo[...])

        def state_block(i, carry):
            mine = pl.ds(pl.multiple_of(i * TAPER_BLOCK, TAPER_BLOCK), TAPER_BLOCK)
            state[mine, :] = updated(state[mine, :], tw_state[k, pl.ds(i, 1), :])
            return carry

        lax.fori_loop(0, state.shape[0] // TAPER_BLOCK, state_block, 0)
        groups = tw_obs.shape[1]
        high = obs.shape[0] // groups
        for g in range(groups):
            mine = slice(g * high, (g + 1) * high)
            obs[mine, :] = updated(obs[mine, :], tw_obs[k, g : g + 1, :])

        def later(i, carry):
            which = i // blocks
            mine = pl.ds(pl.multiple_of(lax.rem(i, blocks) * TAPER_BLOCK, TAPER_BLOCK), TAPER_BLOCK)
            batch[which, mine, :] = updated(batch[which, mine, :], tw_batch[k, pl.ds(i, 1), :])
            return carry

        lax.fori_loop((k + 1) * blocks, steps * blocks, later, 0)
        return carry

    lax.fori_loop(0, steps, one_batch, 0)


def analyse(members, state, obs, batch, tw_state, tw_obs, tw_batch):
    steps, size, width = batch.shape
    blocks = size // TAPER_BLOCK
    vmem = pl.BlockSpec(memory_space=pltpu.VMEM)

    def kernel(*refs):
        analysis_kernel(members, *refs)

    return pl.pallas_call(
        kernel,
        out_shape=(jax.ShapeDtypeStruct(state.shape, f32), jax.ShapeDtypeStruct(obs.shape, f32)),
        in_specs=[vmem] * 6,
        out_specs=(vmem, vmem),
        scratch_shapes=[
            pltpu.VMEM(batch.shape, f32),
            pltpu.VMEM((size, size + width), f32),
            pltpu.VMEM((TAPER_BLOCK, 3 * LANES), f32),
            pltpu.VMEM((TAPER_BLOCK, LANES), f32),
            pltpu.VMEM((blocks, TAPER_BLOCK, LANES), f32),
            pltpu.VMEM((size, members), bf16),
            pltpu.VMEM((size, members), bf16),
            pltpu.VMEM((size, width), f32),
            pltpu.VMEM((size, width), bf16),
            pltpu.VMEM((size, width), bf16),
        ],
        compiler_params=pltpu.CompilerParams(vmem_limit_bytes=48 * 1024 * 1024),
    )(state, obs, batch, tw_state, tw_obs, tw_batch)


def spread_kernel(mesh_axes, share, out, landed, *sems):
    (sum_send, sum_recv, shard_send, shard_recv, peer_send, peer_recv, pair_send, pair_recv) = sems
    regions, shards = (lax.axis_size(name) for name in mesh_axes)
    g, s = (lax.axis_index(name) for name in mesh_axes)
    half = regions // 2
    pair = g + 1 - 2 * lax.rem(g, 2)

    def copy(src, dst, send, recv, device):
        return pltpu.make_async_remote_copy(
            src_ref=src, dst_ref=dst, send_sem=send, recv_sem=recv, device_id=device, device_id_type=pl.DeviceIdType.MESH
        )

    barrier = pltpu.get_barrier_semaphore()
    for o in range(1, regions):
        pl.semaphore_signal(barrier, inc=1, device_id=(lax.rem(g + o, regions), s), device_id_type=pl.DeviceIdType.MESH)
    for o in range(1, shards):
        pl.semaphore_signal(barrier, inc=1, device_id=(g, lax.rem(s + o, shards)), device_id_type=pl.DeviceIdType.MESH)
    pl.semaphore_wait(barrier, regions + shards - 2)

    sums = []
    for o in range(1, regions):
        to = lax.rem(g + o, regions)
        sums.append(copy(share.at[to], landed.at[o - 1], sum_send.at[o - 1], sum_recv.at[o - 1], (to, s)))
        sums[-1].start()
    total = share[g]
    for o in range(1, regions):
        sums[o - 1].wait_recv()
        total = total + landed[o - 1]
    out[g, s] = total

    along = []
    for o in range(1, shards):
        to = lax.rem(s + o, shards)
        along.append(copy(out.at[g, s], out.at[g, s], shard_send.at[o - 1], shard_recv.at[o - 1], (g, to)))
        along[-1].start()
    for c in along:
        c.wait_recv()

    peers = []
    for o in range(1, half):
        to = lax.rem(g + 2 * o, regions)
        peers.append(copy(out.at[g], out.at[g], peer_send.at[o - 1], peer_recv.at[o - 1], (to, s)))
        peers[-1].start()
    pairs = [copy(out.at[g], out.at[g], pair_send.at[0], pair_recv.at[0], (pair, s))]
    pairs[0].start()
    for o in range(1, half):
        peers[o - 1].wait_recv()
        source = lax.rem(g + regions - 2 * o, regions)
        pairs.append(copy(out.at[source], out.at[source], pair_send.at[o], pair_recv.at[o], (pair, s)))
        pairs[-1].start()
    for c in pairs:
        c.wait_recv()
    for c in sums + along + peers + pairs:
        c.wait_send()


def spread(share):
    axes = ("region", "shard")
    regions, shards = (lax.axis_size(name) for name in axes)
    counts = (regions - 1, regions - 1, shards - 1, shards - 1, regions // 2 - 1, regions // 2 - 1, regions // 2, regions // 2)
    vmem = pl.BlockSpec(memory_space=pltpu.VMEM)

    def kernel(*refs):
        spread_kernel(axes, *refs)

    return pl.pallas_call(
        kernel,
        out_shape=jax.ShapeDtypeStruct((regions, shards) + share.shape[1:], f32),
        in_specs=[vmem],
        out_specs=vmem,
        scratch_shapes=[pltpu.VMEM((regions - 1,) + share.shape[1:], f32)]
        + [pltpu.SemaphoreType.DMA((n,)) for n in counts],
        compiler_params=pltpu.CompilerParams(
            collective_id=0, has_side_effects=True, vmem_limit_bytes=32 * 1024 * 1024
        ),
    )(share)


def lookup(levels, index):
    onehot = (index[..., None] == jnp.arange(levels.shape[0], dtype=jnp.int32)).astype(f32)
    return jnp.sum(onehot * levels, axis=-1)


def per_device(
    state_anom, state_mean, obs_anom, obs_depart, obs_var, taper_levels, state_taper, obs_taper, batch_order
):
    region, shard = lax.axis_index("region"), lax.axis_index("shard")
    per_region, pieces, members = obs_anom.shape
    steps = batch_order.shape[0]
    size = pieces * lax.axis_size("shard")
    blocks = size // TAPER_BLOCK

    def columns(weights):
        return jnp.repeat(weights, TAPER_BLOCK, axis=-1) / (members - 1)

    wanted = (batch_order[:, None] * blocks + jnp.arange(blocks, dtype=jnp.int32)).reshape(-1)
    state_weights = lookup(taper_levels, jnp.take(state_taper, wanted, axis=1))
    tw_state = columns(state_weights.reshape(-1, steps, blocks)).transpose(1, 0, 2)
    obs_weights = lookup(taper_levels, jnp.take(obs_taper, wanted, axis=1))
    high = min(pieces, TAPER_BLOCK)
    group_rows = jnp.arange(per_region * pieces // high, dtype=jnp.int32) * high
    group_block = (group_rows // pieces * size + shard * pieces + group_rows % pieces) // TAPER_BLOCK
    mine = jnp.take(obs_weights, group_block, axis=0)
    tw_obs = columns(mine.reshape(-1, steps, blocks)).transpose(1, 0, 2)

    regions, shards = lax.axis_size("region"), lax.axis_size("shard")
    halves = members // LANES

    def filled(rows):
        return jnp.pad(rows, ((0, 0), (0, LANES - rows.shape[1])))[:, None]

    first_group = mine[:: pieces // high]
    small = jnp.concatenate(
        [filled(obs_depart), filled(obs_var), filled(first_group), jnp.zeros((per_region, 5, LANES), f32)], axis=1
    )
    table = jnp.concatenate([obs_anom[:, :, h * LANES : (h + 1) * LANES] for h in range(halves)] + [small], axis=1)
    share = jnp.take(table, batch_order % per_region, axis=0)
    owned = (batch_order // per_region == region)[:, None, None]
    share = jnp.where(owned, share, 0.0).reshape(-1, LANES)
    per_step = halves * pieces + 8
    chunk = -(-steps * per_step // (8 * regions)) * 8
    share = jnp.pad(share, ((0, chunk * regions - steps * per_step), (0, 0))).reshape(regions, chunk, LANES)
    spreaded = spread(share).transpose(1, 0, 2, 3).reshape(shards, regions * chunk, LANES)
    spreaded = spreaded[:, : steps * per_step].reshape(shards, steps, per_step, LANES)
    anomalies = [
        spreaded[:, :, h * pieces : (h + 1) * pieces].transpose(1, 0, 2, 3).reshape(steps, size, LANES)
        for h in range(halves)
    ]
    small = spreaded[:, :, halves * pieces :]
    columns_in = small[:, :, :2, :pieces].transpose(1, 0, 3, 2).reshape(steps, size, 2)
    batch = jnp.concatenate(anomalies + [jnp.pad(columns_in, ((0, 0), (0, 0), (0, LANES - 2)))], axis=-1)

    between = small[:: TAPER_BLOCK // pieces, :, 2, : steps * blocks].transpose(1, 0, 2)
    tw_batch = columns(between.reshape(steps * blocks, steps, blocks)).transpose(1, 0, 2)

    def widened(rows, column):
        pad = jnp.zeros((rows.shape[0], LANES - 1), f32)
        return jnp.concatenate([rows, column[:, None], pad], axis=1)

    state, obs = analyse(
        members,
        widened(state_anom, -state_mean),
        widened(obs_anom.reshape(-1, members), obs_depart.reshape(-1)),
        batch,
        tw_state,
        tw_obs,
        tw_batch,
    )
    return (
        state[:, :members],
        -state[:, members],
        obs[:, :members].reshape(obs_anom.shape),
        obs[:, members].reshape(obs_depart.shape),
    )


def solution(mesh):
    placed = (
        P(("region", "shard"), None),
        P(("region", "shard")),
        P("region", "shard", None),
        P("region", "shard"),
        P("region", "shard"),
        P(),
        P(("region", "shard"), None),
        P("region", None),
        P(),
    )
    return jax.shard_map(
        per_device,
        mesh=mesh,
        in_specs=placed,
        out_specs=(
            P(("region", "shard"), None),
            P(("region", "shard")),
            P("region", "shard", None),
            P("region", "shard"),
        ),
        check_vma=False,
    )
```

```python
import math

import jax
import jax.numpy as jnp
from jax import lax
from jax.experimental import pallas as pl
from jax.experimental.pallas import tpu as pltpu
from jax.sharding import PartitionSpec as P

TAPER_BLOCK = 128
LANES = 128
PANEL = 16
highest = lax.Precision.HIGHEST
f32 = jnp.float32
bf16 = jnp.bfloat16


def dot(a, b, dims=((1,), (0,))):
    return lax.dot_general(a, b, (dims, ((), ())), precision=highest, preferred_element_type=f32)


def split2(x):
    hi = x.astype(bf16)
    return hi, (x - hi.astype(f32)).astype(bf16)


def split3(x):
    hi = x.astype(bf16).astype(f32)
    rest = x - hi
    mid = rest.astype(bf16).astype(f32)
    return hi, mid, rest - mid


def dot3(a, b_hi, b_lo, dims=((1,), (0,))):
    hi, lo = split2(a)

    def one(u, v):
        return lax.dot_general(u, v, (dims, ((), ())), preferred_element_type=f32)

    return one(hi, b_hi) + (one(hi, b_lo) + one(lo, b_hi))


def factor_block(sgh, roots):
    rows = lax.broadcasted_iota(jnp.int32, (PANEL, LANES), 0)
    for start in range(0, TAPER_BLOCK, PANEL):
        panel = sgh[start : start + PANEL, :]
        cols = [
            jnp.broadcast_to(panel[:, start + t : start + t + 1], (PANEL, LANES))
            for t in range(PANEL)
        ]
        parts = [panel[:, LANES * q : LANES * (q + 1)] for q in range(3)]
        root = roots[start : start + PANEL, :]
        for r in range(PANEL):
            mine = cols[r]
            pivot = mine[r : r + 1, :]
            inv = lax.rsqrt(pivot)
            inv_pivot = inv * inv
            for t in range(r + 1, PANEL):
                cols[t] = cols[t] - (mine * mine[t : t + 1, :]) * inv_pivot
            column = mine * inv
            below = jnp.where(rows > r, column, 0.0)
            shifted = 1.0 / (pivot * inv + root[r : r + 1, :])
            for q, scale in enumerate((inv, inv, shifted)):
                done = parts[q][r : r + 1, :] * scale
                parts[q] = jnp.where(rows == r, done, parts[q] - below * done)
        solved = jnp.concatenate(parts, axis=1)
        sgh[start : start + PANEL, :] = solved
        after = start + PANEL
        if after < TAPER_BLOCK:
            a, b, c = split3(parts[0])
            left = jnp.concatenate([a, a, b, a, b, c, jnp.zeros((32, LANES), f32)], axis=0)
            x, y, z = (v.astype(bf16) for v in split3(solved))
            right = jnp.concatenate([x, y, x, z, y, x, jnp.zeros((32, 3 * LANES), bf16)], axis=0)
            left = left.T[after:, :].astype(bf16)
            sgh[after:, :] = sgh[after:, :] - jnp.dot(left, right, preferred_element_type=f32)


def analysis_kernel(
    members, state_in, mean_in, obs_in, depart_in, batch_in, tw_state, tw_obs, tw_batch, state, mean, obs, depart, batch, work, sgh, roots, inverses, y_hi, y_lo, z, z_hi, z_lo
):
    steps, size, width = batch_in.shape
    blocks = size // TAPER_BLOCK
    state[...] = state_in[...]
    mean[...] = mean_in[...]
    obs[...] = obs_in[...]
    depart[...] = depart_in[...]
    state_rows = TAPER_BLOCK * math.gcd(state.shape[0] // TAPER_BLOCK, 4)
    for k in range(steps):
        batch[k] = batch_in[k]
    eye = (
        lax.broadcasted_iota(jnp.int32, (TAPER_BLOCK, LANES), 0)
        == lax.broadcasted_iota(jnp.int32, (TAPER_BLOCK, LANES), 1)
    ).astype(f32)
    extra = size + members

    def one_batch(k, carry):
        y = batch[k, :, :members]
        hi, lo = split2(y)
        y_hi[...] = hi
        y_lo[...] = lo
        work[:, size:] = batch[k]
        for j in range(blocks):
            here = y[j * TAPER_BLOCK : (j + 1) * TAPER_BLOCK]
            work[j * TAPER_BLOCK : (j + 1) * TAPER_BLOCK, :size] = dot(here, y, ((1,), (1,))) / (members - 1)

        def eliminate(j, carry):
            top = pl.multiple_of(j * TAPER_BLOCK, TAPER_BLOCK)
            mine = pl.ds(top, TAPER_BLOCK)
            variance = jnp.broadcast_to(batch[k, mine, members + 1 : members + 2], (TAPER_BLOCK, LANES))
            roots[...] = jnp.sqrt(variance)
            sgh[:, :LANES] = work[mine, mine] + eye * variance
            sgh[:, LANES : 2 * LANES] = eye
            sgh[:, 2 * LANES :] = eye
            factor_block(sgh, roots)
            inverse = sgh[:, LANES : 2 * LANES]
            inverses[j] = inverse
            work[mine, :size] = dot(inverse, work[mine, :size])
            work[mine, size:extra] = dot(sgh[:, 2 * LANES :], work[mine, size:extra])
            work[mine, extra:] = dot(inverse, work[mine, extra:])

            for last in range(blocks - 1):
                @pl.when(j == last)
                def trail(edge=(last + 1) * TAPER_BLOCK):
                    factor = work[mine, edge:size].T
                    work[edge:, edge:] = work[edge:, edge:] - dot(factor, work[mine, edge:])

            return carry

        lax.fori_loop(0, blocks, eliminate, 0)

        for j in reversed(range(blocks)):
            mine, edge = slice(j * TAPER_BLOCK, (j + 1) * TAPER_BLOCK), (j + 1) * TAPER_BLOCK
            acc = work[mine, size:]
            if edge < size:
                acc = acc - dot(work[mine, edge:size], z[edge:, :])
            z[mine, :] = dot(inverses[j].T, acc)
        for j in range(blocks):
            mine = slice(j * TAPER_BLOCK, (j + 1) * TAPER_BLOCK)
            tail = jnp.broadcast_to(z[mine, members : members + 1], (TAPER_BLOCK, LANES))
            full = jnp.concatenate([z[mine, :members], tail], axis=1)
            hi, lo = split2(full)
            z_hi[mine, :] = hi
            z_lo[mine, :] = lo

        def change(x, weights):
            covar = dot3(x, y_hi[...], y_lo[...], ((1,), (1,)))
            high = x.shape[0] // weights.shape[0]
            parts = [covar[g * high : (g + 1) * high] * weights[g : g + 1, :] for g in range(weights.shape[0])]
            covar = jnp.concatenate(parts, axis=0) if len(parts) > 1 else parts[0]
            return dot3(covar, z_hi[...], z_lo[...])

        def picked(delta, g, high):
            tail = delta[g * high : (g + 1) * high, members : members + high]
            return jnp.sum(tail * eye[:high, :high], axis=0, keepdims=True)

        several = state_rows // TAPER_BLOCK
        for first in range(0, tw_state.shape[1], several):
            mine = slice(first * TAPER_BLOCK, first * TAPER_BLOCK + state_rows)
            delta = change(state[mine, :], tw_state[k, first : first + several, :])
            state[mine, :] = state[mine, :] - delta[:, :members]
            for g in range(several):
                one = slice(first + g, first + g + 1)
                mean[one, :] = mean[one, :] + picked(delta, g, TAPER_BLOCK)
        groups, high = depart.shape
        delta = change(obs[...], tw_obs[k])
        obs[...] = obs[...] - delta[:, :members]
        for g in range(groups):
            depart[g : g + 1, :] = depart[g : g + 1, :] - picked(delta, g, high)

        lane = lax.broadcasted_iota(jnp.int32, (size, LANES), 1)
        for i in range(1, steps):
            @pl.when(i > k)
            def later(i=i):
                delta = change(batch[i, :, :members], tw_batch[k, i * blocks : (i + 1) * blocks, :])
                batch[i, :, :members] = batch[i, :, :members] - delta[:, :members]
                batch[i, :, members:] = batch[i, :, members:] - jnp.where(lane == 0, delta[:, members:], 0.0)

        return carry

    lax.fori_loop(0, steps, one_batch, 0)


def analyse(members, state, mean, obs, depart, batch, tw_state, tw_obs, tw_batch):
    steps, size, width = batch.shape
    blocks = size // TAPER_BLOCK
    vmem = pl.BlockSpec(memory_space=pltpu.VMEM)

    def kernel(*refs):
        analysis_kernel(members, *refs)

    return pl.pallas_call(
        kernel,
        out_shape=tuple(jax.ShapeDtypeStruct(v.shape, f32) for v in (state, mean, obs, depart)),
        in_specs=[vmem] * 8,
        out_specs=(vmem,) * 4,
        scratch_shapes=[
            pltpu.VMEM(batch.shape, f32),
            pltpu.VMEM((size, size + width), f32),
            pltpu.VMEM((TAPER_BLOCK, 3 * LANES), f32),
            pltpu.VMEM((TAPER_BLOCK, LANES), f32),
            pltpu.VMEM((blocks, TAPER_BLOCK, LANES), f32),
            pltpu.VMEM((size, members), bf16),
            pltpu.VMEM((size, members), bf16),
            pltpu.VMEM((size, width), f32),
            pltpu.VMEM((size, width), bf16),
            pltpu.VMEM((size, width), bf16),
        ],
        compiler_params=pltpu.CompilerParams(vmem_limit_bytes=48 * 1024 * 1024),
    )(state, mean, obs, depart, batch, tw_state, tw_obs, tw_batch)


def spread_kernel(mesh_axes, share, out, landed, *sems):
    (sum_send, sum_recv, shard_send, shard_recv, peer_send, peer_recv, pair_send, pair_recv) = sems
    regions, shards = (lax.axis_size(name) for name in mesh_axes)
    g, s = (lax.axis_index(name) for name in mesh_axes)
    half = regions // 2
    pair = g + 1 - 2 * lax.rem(g, 2)

    def copy(src, dst, send, recv, device):
        return pltpu.make_async_remote_copy(
            src_ref=src, dst_ref=dst, send_sem=send, recv_sem=recv, device_id=device, device_id_type=pl.DeviceIdType.MESH
        )

    barrier = pltpu.get_barrier_semaphore()
    for o in range(1, regions):
        pl.semaphore_signal(barrier, inc=1, device_id=(lax.rem(g + o, regions), s), device_id_type=pl.DeviceIdType.MESH)
    for o in range(1, shards):
        pl.semaphore_signal(barrier, inc=1, device_id=(g, lax.rem(s + o, shards)), device_id_type=pl.DeviceIdType.MESH)
    pl.semaphore_wait(barrier, regions + shards - 2)

    sums = []
    for o in range(1, regions):
        to = lax.rem(g + o, regions)
        sums.append(copy(share.at[to], landed.at[o - 1], sum_send.at[o - 1], sum_recv.at[o - 1], (to, s)))
        sums[-1].start()
    total = share[g]
    for o in range(1, regions):
        sums[o - 1].wait_recv()
        total = total + landed[o - 1]
    out[g, s] = total

    along = []
    for o in range(1, shards):
        to = lax.rem(s + o, shards)
        along.append(copy(out.at[g, s], out.at[g, s], shard_send.at[o - 1], shard_recv.at[o - 1], (g, to)))
        along[-1].start()
    for c in along:
        c.wait_recv()

    peers = []
    for o in range(1, half):
        to = lax.rem(g + 2 * o, regions)
        peers.append(copy(out.at[g], out.at[g], peer_send.at[o - 1], peer_recv.at[o - 1], (to, s)))
        peers[-1].start()
    pairs = [copy(out.at[g], out.at[g], pair_send.at[0], pair_recv.at[0], (pair, s))]
    pairs[0].start()
    for o in range(1, half):
        peers[o - 1].wait_recv()
        source = lax.rem(g + regions - 2 * o, regions)
        pairs.append(copy(out.at[source], out.at[source], pair_send.at[o], pair_recv.at[o], (pair, s)))
        pairs[-1].start()
    for c in pairs:
        c.wait_recv()
    for c in sums + along + peers + pairs:
        c.wait_send()


def spread(share):
    axes = ("region", "shard")
    regions, shards = (lax.axis_size(name) for name in axes)
    counts = (regions - 1, regions - 1, shards - 1, shards - 1, regions // 2 - 1, regions // 2 - 1, regions // 2, regions // 2)
    vmem = pl.BlockSpec(memory_space=pltpu.VMEM)

    def kernel(*refs):
        spread_kernel(axes, *refs)

    return pl.pallas_call(
        kernel,
        out_shape=jax.ShapeDtypeStruct((regions, shards) + share.shape[1:], f32),
        in_specs=[vmem],
        out_specs=vmem,
        scratch_shapes=[pltpu.VMEM((regions - 1,) + share.shape[1:], f32)]
        + [pltpu.SemaphoreType.DMA((n,)) for n in counts],
        compiler_params=pltpu.CompilerParams(
            collective_id=0, has_side_effects=True, vmem_limit_bytes=32 * 1024 * 1024
        ),
    )(share)


def lookup(levels, index):
    onehot = (index[..., None] == jnp.arange(levels.shape[0], dtype=jnp.int32)).astype(f32)
    return jnp.sum(onehot * levels, axis=-1)


def per_device(
    state_anom, state_mean, obs_anom, obs_depart, obs_var, taper_levels, state_taper, obs_taper, batch_order
):
    region, shard = lax.axis_index("region"), lax.axis_index("shard")
    per_region, pieces, members = obs_anom.shape
    steps = batch_order.shape[0]
    size = pieces * lax.axis_size("shard")
    blocks = size // TAPER_BLOCK

    def columns(weights):
        return jnp.repeat(weights, TAPER_BLOCK, axis=-1) / (members - 1)

    wanted = (batch_order[:, None] * blocks + jnp.arange(blocks, dtype=jnp.int32)).reshape(-1)
    state_weights = lookup(taper_levels, jnp.take(state_taper, wanted, axis=1))
    tw_state = columns(state_weights.reshape(-1, steps, blocks)).transpose(1, 0, 2)
    obs_weights = lookup(taper_levels, jnp.take(obs_taper, wanted, axis=1))
    high = min(pieces, TAPER_BLOCK)
    group_rows = jnp.arange(per_region * pieces // high, dtype=jnp.int32) * high
    group_block = (group_rows // pieces * size + shard * pieces + group_rows % pieces) // TAPER_BLOCK
    mine = jnp.take(obs_weights, group_block, axis=0)
    tw_obs = columns(mine.reshape(-1, steps, blocks)).transpose(1, 0, 2)

    regions, shards = lax.axis_size("region"), lax.axis_size("shard")
    halves = members // LANES

    def filled(rows):
        return jnp.pad(rows, ((0, 0), (0, LANES - rows.shape[1])))[:, None]

    first_group = mine[:: pieces // high]
    small = jnp.concatenate(
        [filled(obs_depart), filled(obs_var), filled(first_group), jnp.zeros((per_region, 5, LANES), f32)], axis=1
    )
    table = jnp.concatenate([obs_anom[:, :, h * LANES : (h + 1) * LANES] for h in range(halves)] + [small], axis=1)
    share = jnp.take(table, batch_order % per_region, axis=0)
    owned = (batch_order // per_region == region)[:, None, None]
    share = jnp.where(owned, share, 0.0).reshape(-1, LANES)
    per_step = halves * pieces + 8
    chunk = -(-steps * per_step // (8 * regions)) * 8
    share = jnp.pad(share, ((0, chunk * regions - steps * per_step), (0, 0))).reshape(regions, chunk, LANES)
    spreaded = spread(share).transpose(1, 0, 2, 3).reshape(shards, regions * chunk, LANES)
    spreaded = spreaded[:, : steps * per_step].reshape(shards, steps, per_step, LANES)
    anomalies = [
        spreaded[:, :, h * pieces : (h + 1) * pieces].transpose(1, 0, 2, 3).reshape(steps, size, LANES)
        for h in range(halves)
    ]
    small = spreaded[:, :, halves * pieces :]
    columns_in = small[:, :, :2, :pieces].transpose(1, 0, 3, 2).reshape(steps, size, 2)
    batch = jnp.concatenate(anomalies + [jnp.pad(columns_in, ((0, 0), (0, 0), (0, LANES - 2)))], axis=-1)

    between = small[:: TAPER_BLOCK // pieces, :, 2, : steps * blocks].transpose(1, 0, 2)
    tw_batch = columns(between.reshape(steps * blocks, steps, blocks)).transpose(1, 0, 2)

    state, mean, obs, depart = analyse(
        members,
        state_anom,
        state_mean.reshape(-1, TAPER_BLOCK),
        obs_anom.reshape(-1, members),
        obs_depart.reshape(-1, high),
        batch,
        tw_state,
        tw_obs,
        tw_batch,
    )
    return state, mean.reshape(-1), obs.reshape(obs_anom.shape), depart.reshape(obs_depart.shape)


def solution(mesh):
    placed = (
        P(("region", "shard"), None),
        P(("region", "shard")),
        P("region", "shard", None),
        P("region", "shard"),
        P("region", "shard"),
        P(),
        P(("region", "shard"), None),
        P("region", None),
        P(),
    )
    return jax.shard_map(
        per_device,
        mesh=mesh,
        in_specs=placed,
        out_specs=(
            P(("region", "shard"), None),
            P(("region", "shard")),
            P("region", "shard", None),
            P("region", "shard"),
        ),
        check_vma=False,
    )
```

```python
import math

import jax
import jax.numpy as jnp
from jax import lax
from jax.experimental import pallas as pl
from jax.experimental.pallas import tpu as pltpu
from jax.sharding import PartitionSpec as P

TAPER_BLOCK = 128
LANES = 128
PANEL = 16
HALF = 8
highest = lax.Precision.HIGHEST
f32 = jnp.float32
bf16 = jnp.bfloat16


def dot(a, b, dims=((1,), (0,))):
    return lax.dot_general(a, b, (dims, ((), ())), precision=highest, preferred_element_type=f32)


def split2(x):
    hi = x.astype(bf16)
    return hi, (x - hi.astype(f32)).astype(bf16)


def split3(x):
    hi = x.astype(bf16).astype(f32)
    rest = x - hi
    mid = rest.astype(bf16).astype(f32)
    return hi, mid, rest - mid


def dot3(a, b_hi, b_lo, dims=((1,), (0,))):
    hi, lo = split2(a)

    def one(u, v):
        return lax.dot_general(u, v, (dims, ((), ())), preferred_element_type=f32)

    return one(hi, b_hi) + (one(hi, b_lo) + one(lo, b_hi))


def factor_block(sgh, roots):
    rows = lax.broadcasted_iota(jnp.int32, (HALF, LANES), 0)
    halves = PANEL // HALF
    for start in range(0, TAPER_BLOCK, PANEL):
        panel = [sgh[start + HALF * h : start + HALF * (h + 1), :] for h in range(halves)]
        cols = [
            [
                jnp.broadcast_to(panel[h][:, start + t : start + t + 1], (HALF, LANES)) if h >= t // HALF else None
                for h in range(halves)
            ]
            for t in range(PANEL)
        ]
        parts = [[panel[h][:, LANES * q : LANES * (q + 1)] for h in range(halves)] for q in range(3)]
        root = [roots[start + HALF * h : start + HALF * (h + 1), :] for h in range(halves)]
        for r in range(PANEL):
            mine, home, at = cols[r], r // HALF, slice(r % HALF, r % HALF + 1)
            pivot = mine[home][at, :]
            inv = lax.rsqrt(pivot)
            inv_pivot = inv * inv
            for h in range(home, halves):
                scaled = mine[h] * inv_pivot
                for t in range(r + 1, PANEL):
                    if h >= t // HALF:
                        row = mine[t // HALF][t % HALF : t % HALF + 1, :]
                        if t == r + 1:
                            cols[t][h] = cols[t][h] - (mine[h] * row) * inv_pivot
                        else:
                            cols[t][h] = cols[t][h] - scaled * row
            shifted = 1.0 / (pivot * inv + root[home][at, :])
            for q, scale in enumerate((inv, inv, shifted)):
                done = parts[q][home][at, :] * scale
                for h in range(home, halves):
                    column = mine[h] * inv
                    if h == home:
                        below = jnp.where(rows > r % HALF, column, 0.0)
                        parts[q][h] = jnp.where(rows == r % HALF, done, parts[q][h] - below * done)
                    else:
                        parts[q][h] = parts[q][h] - column * done
        parts = [jnp.concatenate(part, axis=0) for part in parts]
        solved = jnp.concatenate(parts, axis=1)
        sgh[start : start + PANEL, :] = solved
        after = start + PANEL
        if after < TAPER_BLOCK:
            a, b, c = split3(parts[0])
            left = jnp.concatenate([a, a, b, a, b, c, jnp.zeros((32, LANES), f32)], axis=0)
            x, y, z = (v.astype(bf16) for v in split3(solved))
            right = jnp.concatenate([x, y, x, z, y, x, jnp.zeros((32, 3 * LANES), bf16)], axis=0)
            left = left.T[after:, :].astype(bf16)
            sgh[after:, :] = sgh[after:, :] - jnp.dot(left, right, preferred_element_type=f32)


def analysis_kernel(
    members, state_in, mean_in, obs_in, depart_in, batch_in, tw_state, tw_obs, tw_batch, state, mean, obs, depart, batch, work, sgh, roots, inverses, y_hi, y_lo, z, z_hi, z_lo
):
    steps, size, width = batch_in.shape
    blocks = size // TAPER_BLOCK
    state[...] = state_in[...]
    mean[...] = mean_in[...]
    obs[...] = obs_in[...]
    depart[...] = depart_in[...]
    state_rows = TAPER_BLOCK * math.gcd(state.shape[0] // TAPER_BLOCK, 4)
    for k in range(steps):
        batch[k] = batch_in[k]
    eye = (
        lax.broadcasted_iota(jnp.int32, (TAPER_BLOCK, LANES), 0)
        == lax.broadcasted_iota(jnp.int32, (TAPER_BLOCK, LANES), 1)
    ).astype(f32)
    extra = size + members

    def one_batch(k, carry):
        y = batch[k, :, :members]
        hi, lo = split2(y)
        y_hi[...] = hi
        y_lo[...] = lo
        work[:, size:] = batch[k]
        for j in range(blocks):
            here = y[j * TAPER_BLOCK : (j + 1) * TAPER_BLOCK]
            work[j * TAPER_BLOCK : (j + 1) * TAPER_BLOCK, :size] = dot(here, y, ((1,), (1,))) / (members - 1)

        def eliminate(j, carry):
            top = pl.multiple_of(j * TAPER_BLOCK, TAPER_BLOCK)
            mine = pl.ds(top, TAPER_BLOCK)
            variance = jnp.broadcast_to(batch[k, mine, members + 1 : members + 2], (TAPER_BLOCK, LANES))
            roots[...] = jnp.sqrt(variance)
            sgh[:, :LANES] = work[mine, mine] + eye * variance
            sgh[:, LANES : 2 * LANES] = eye
            sgh[:, 2 * LANES :] = eye
            factor_block(sgh, roots)
            inverse = sgh[:, LANES : 2 * LANES]
            inverses[j] = inverse
            work[mine, :size] = dot(inverse, work[mine, :size])
            work[mine, size:extra] = dot(sgh[:, 2 * LANES :], work[mine, size:extra])
            work[mine, extra:] = dot(inverse, work[mine, extra:])

            for last in range(blocks - 1):
                @pl.when(j == last)
                def trail(edge=(last + 1) * TAPER_BLOCK):
                    factor = work[mine, edge:size].T
                    work[edge:, edge:] = work[edge:, edge:] - dot(factor, work[mine, edge:])

            return carry

        lax.fori_loop(0, blocks, eliminate, 0)

        for j in reversed(range(blocks)):
            mine, edge = slice(j * TAPER_BLOCK, (j + 1) * TAPER_BLOCK), (j + 1) * TAPER_BLOCK
            acc = work[mine, size:]
            if edge < size:
                acc = acc - dot(work[mine, edge:size], z[edge:, :])
            z[mine, :] = dot(inverses[j].T, acc)
        for j in range(blocks):
            mine = slice(j * TAPER_BLOCK, (j + 1) * TAPER_BLOCK)
            tail = jnp.broadcast_to(z[mine, members : members + 1], (TAPER_BLOCK, LANES))
            full = jnp.concatenate([z[mine, :members], tail], axis=1)
            hi, lo = split2(full)
            z_hi[mine, :] = hi
            z_lo[mine, :] = lo

        def change(x, weights):
            covar = dot3(x, y_hi[...], y_lo[...], ((1,), (1,)))
            high = x.shape[0] // weights.shape[0]
            parts = [covar[g * high : (g + 1) * high] * weights[g : g + 1, :] for g in range(weights.shape[0])]
            covar = jnp.concatenate(parts, axis=0) if len(parts) > 1 else parts[0]
            return dot3(covar, z_hi[...], z_lo[...])

        def picked(delta, g, high):
            tail = delta[g * high : (g + 1) * high, members : members + high]
            return jnp.sum(tail * eye[:high, :high], axis=0, keepdims=True)

        several = state_rows // TAPER_BLOCK
        for first in range(0, tw_state.shape[1], several):
            mine = slice(first * TAPER_BLOCK, first * TAPER_BLOCK + state_rows)
            delta = change(state[mine, :], tw_state[k, first : first + several, :])
            state[mine, :] = state[mine, :] - delta[:, :members]
            for g in range(several):
                one = slice(first + g, first + g + 1)
                mean[one, :] = mean[one, :] + picked(delta, g, TAPER_BLOCK)
        groups, high = depart.shape
        delta = change(obs[...], tw_obs[k])
        obs[...] = obs[...] - delta[:, :members]
        for g in range(groups):
            depart[g : g + 1, :] = depart[g : g + 1, :] - picked(delta, g, high)

        lane = lax.broadcasted_iota(jnp.int32, (size, LANES), 1)
        for i in range(1, steps):
            @pl.when(i > k)
            def later(i=i):
                delta = change(batch[i, :, :members], tw_batch[k, i * blocks : (i + 1) * blocks, :])
                batch[i, :, :members] = batch[i, :, :members] - delta[:, :members]
                batch[i, :, members:] = batch[i, :, members:] - jnp.where(lane == 0, delta[:, members:], 0.0)

        return carry

    lax.fori_loop(0, steps, one_batch, 0)


def analyse(members, state, mean, obs, depart, batch, tw_state, tw_obs, tw_batch):
    steps, size, width = batch.shape
    blocks = size // TAPER_BLOCK
    vmem = pl.BlockSpec(memory_space=pltpu.VMEM)

    def kernel(*refs):
        analysis_kernel(members, *refs)

    return pl.pallas_call(
        kernel,
        out_shape=tuple(jax.ShapeDtypeStruct(v.shape, f32) for v in (state, mean, obs, depart)),
        in_specs=[vmem] * 8,
        out_specs=(vmem,) * 4,
        scratch_shapes=[
            pltpu.VMEM(batch.shape, f32),
            pltpu.VMEM((size, size + width), f32),
            pltpu.VMEM((TAPER_BLOCK, 3 * LANES), f32),
            pltpu.VMEM((TAPER_BLOCK, LANES), f32),
            pltpu.VMEM((blocks, TAPER_BLOCK, LANES), f32),
            pltpu.VMEM((size, members), bf16),
            pltpu.VMEM((size, members), bf16),
            pltpu.VMEM((size, width), f32),
            pltpu.VMEM((size, width), bf16),
            pltpu.VMEM((size, width), bf16),
        ],
        compiler_params=pltpu.CompilerParams(vmem_limit_bytes=48 * 1024 * 1024),
    )(state, mean, obs, depart, batch, tw_state, tw_obs, tw_batch)


def spread_kernel(mesh_axes, share, out, landed, *sems):
    (sum_send, sum_recv, shard_send, shard_recv, peer_send, peer_recv, pair_send, pair_recv) = sems
    regions, shards = (lax.axis_size(name) for name in mesh_axes)
    g, s = (lax.axis_index(name) for name in mesh_axes)
    half = regions // 2
    pair = g + 1 - 2 * lax.rem(g, 2)

    def copy(src, dst, send, recv, device):
        return pltpu.make_async_remote_copy(
            src_ref=src, dst_ref=dst, send_sem=send, recv_sem=recv, device_id=device, device_id_type=pl.DeviceIdType.MESH
        )

    barrier = pltpu.get_barrier_semaphore()
    for o in range(1, regions):
        pl.semaphore_signal(barrier, inc=1, device_id=(lax.rem(g + o, regions), s), device_id_type=pl.DeviceIdType.MESH)
    for o in range(1, shards):
        pl.semaphore_signal(barrier, inc=1, device_id=(g, lax.rem(s + o, shards)), device_id_type=pl.DeviceIdType.MESH)
    pl.semaphore_wait(barrier, regions + shards - 2)

    sums = []
    for o in range(1, regions):
        to = lax.rem(g + o, regions)
        sums.append(copy(share.at[to], landed.at[o - 1], sum_send.at[o - 1], sum_recv.at[o - 1], (to, s)))
        sums[-1].start()
    total = share[g]
    for o in range(1, regions):
        sums[o - 1].wait_recv()
        total = total + landed[o - 1]
    out[g, s] = total

    along = []
    for o in range(1, shards):
        to = lax.rem(s + o, shards)
        along.append(copy(out.at[g, s], out.at[g, s], shard_send.at[o - 1], shard_recv.at[o - 1], (g, to)))
        along[-1].start()
    for c in along:
        c.wait_recv()

    peers = []
    for o in range(1, half):
        to = lax.rem(g + 2 * o, regions)
        peers.append(copy(out.at[g], out.at[g], peer_send.at[o - 1], peer_recv.at[o - 1], (to, s)))
        peers[-1].start()
    pairs = [copy(out.at[g], out.at[g], pair_send.at[0], pair_recv.at[0], (pair, s))]
    pairs[0].start()
    for o in range(1, half):
        peers[o - 1].wait_recv()
        source = lax.rem(g + regions - 2 * o, regions)
        pairs.append(copy(out.at[source], out.at[source], pair_send.at[o], pair_recv.at[o], (pair, s)))
        pairs[-1].start()
    for c in pairs:
        c.wait_recv()
    for c in sums + along + peers + pairs:
        c.wait_send()


def spread(share):
    axes = ("region", "shard")
    regions, shards = (lax.axis_size(name) for name in axes)
    counts = (regions - 1, regions - 1, shards - 1, shards - 1, regions // 2 - 1, regions // 2 - 1, regions // 2, regions // 2)
    vmem = pl.BlockSpec(memory_space=pltpu.VMEM)

    def kernel(*refs):
        spread_kernel(axes, *refs)

    return pl.pallas_call(
        kernel,
        out_shape=jax.ShapeDtypeStruct((regions, shards) + share.shape[1:], f32),
        in_specs=[vmem],
        out_specs=vmem,
        scratch_shapes=[pltpu.VMEM((regions - 1,) + share.shape[1:], f32)]
        + [pltpu.SemaphoreType.DMA((n,)) for n in counts],
        compiler_params=pltpu.CompilerParams(
            collective_id=0, has_side_effects=True, vmem_limit_bytes=32 * 1024 * 1024
        ),
    )(share)


def lookup(levels, index):
    onehot = (index[..., None] == jnp.arange(levels.shape[0], dtype=jnp.int32)).astype(f32)
    return jnp.sum(onehot * levels, axis=-1)


def per_device(
    state_anom, state_mean, obs_anom, obs_depart, obs_var, taper_levels, state_taper, obs_taper, batch_order
):
    region, shard = lax.axis_index("region"), lax.axis_index("shard")
    per_region, pieces, members = obs_anom.shape
    steps = batch_order.shape[0]
    size = pieces * lax.axis_size("shard")
    blocks = size // TAPER_BLOCK

    def columns(weights):
        return jnp.repeat(weights, TAPER_BLOCK, axis=-1) / (members - 1)

    high = min(pieces, TAPER_BLOCK)
    group_rows = jnp.arange(per_region * pieces // high, dtype=jnp.int32) * high
    group_block = (group_rows // pieces * size + shard * pieces + group_rows % pieces) // TAPER_BLOCK
    index = jnp.concatenate([state_taper, jnp.take(obs_taper, group_block, axis=0)], axis=0)
    index = jnp.take(index.reshape(index.shape[0], -1, blocks), batch_order, axis=1)
    weights = lookup(taper_levels, index)
    spread_weights = columns(weights).transpose(1, 0, 2)
    tw_state = spread_weights[:, : state_taper.shape[0]]
    tw_obs = spread_weights[:, state_taper.shape[0] :]
    mine = weights[state_taper.shape[0] :].reshape(-1, steps * blocks)

    regions, shards = lax.axis_size("region"), lax.axis_size("shard")
    halves = members // LANES

    def filled(rows):
        return jnp.pad(rows, ((0, 0), (0, LANES - rows.shape[1])))[:, None]

    first_group = mine[:: pieces // high]
    small = jnp.concatenate(
        [filled(obs_depart), filled(obs_var), filled(first_group), jnp.zeros((per_region, 5, LANES), f32)], axis=1
    )
    table = jnp.concatenate([obs_anom[:, :, h * LANES : (h + 1) * LANES] for h in range(halves)] + [small], axis=1)
    share = jnp.take(table, batch_order % per_region, axis=0)
    owned = (batch_order // per_region == region)[:, None, None]
    share = jnp.where(owned, share, 0.0).reshape(-1, LANES)
    per_step = halves * pieces + 8
    chunk = -(-steps * per_step // (8 * regions)) * 8
    share = jnp.pad(share, ((0, chunk * regions - steps * per_step), (0, 0))).reshape(regions, chunk, LANES)
    spreaded = spread(share).transpose(1, 0, 2, 3).reshape(shards, regions * chunk, LANES)
    spreaded = spreaded[:, : steps * per_step].reshape(shards, steps, per_step, LANES)
    anomalies = [
        spreaded[:, :, h * pieces : (h + 1) * pieces].transpose(1, 0, 2, 3).reshape(steps, size, LANES)
        for h in range(halves)
    ]
    small = spreaded[:, :, halves * pieces :]
    columns_in = small[:, :, :2, :pieces].transpose(1, 0, 3, 2).reshape(steps, size, 2)
    batch = jnp.concatenate(anomalies + [jnp.pad(columns_in, ((0, 0), (0, 0), (0, LANES - 2)))], axis=-1)

    between = small[:: TAPER_BLOCK // pieces, :, 2, : steps * blocks].transpose(1, 0, 2)
    tw_batch = columns(between.reshape(steps * blocks, steps, blocks)).transpose(1, 0, 2)

    state, mean, obs, depart = analyse(
        members,
        state_anom,
        state_mean.reshape(-1, TAPER_BLOCK),
        obs_anom.reshape(-1, members),
        obs_depart.reshape(-1, high),
        batch,
        tw_state,
        tw_obs,
        tw_batch,
    )
    return state, mean.reshape(-1), obs.reshape(obs_anom.shape), depart.reshape(obs_depart.shape)


def solution(mesh):
    placed = (
        P(("region", "shard"), None),
        P(("region", "shard")),
        P("region", "shard", None),
        P("region", "shard"),
        P("region", "shard"),
        P(),
        P(("region", "shard"), None),
        P("region", None),
        P(),
    )
    return jax.shard_map(
        per_device,
        mesh=mesh,
        in_specs=placed,
        out_specs=(
            P(("region", "shard"), None),
            P(("region", "shard")),
            P("region", "shard", None),
            P("region", "shard"),
        ),
        check_vma=False,
    )
```
